32 devices in a mesh: section: 4 (over x, core), lon: 4 (over z), lat: 2 (over y).
Axes of the slice: x: 2, y: 2, z: 4, core: 2. Of those that a mesh axis runs over, the one named last changes fastest.
Arguments:
- inputs: bfloat16 [4, 8, 12, 48, 192], P('section', None, 'lat', 'lon'), may hold values from -6 to 6
- grad_output: bfloat16 [4, 8, 12, 48, 192], P('section', None, 'lat', 'lon'), may hold values from -6 to 6
- norm_gains: float32 [4, 2, 2, 192], P('section'), may hold values from 0.25 to 1.75
- input_weight: bfloat16 [4, 2, 192, 576], P('section'), may hold values from -0.4375 to 0.4375
- output_weight: bfloat16 [4, 2, 192, 192], P('section'), may hold values from -0.4375 to 0.4375
- expand_weight: bfloat16 [4, 2, 192, 768], P('section'), may hold values from -0.4375 to 0.4375
- reduce_weight: bfloat16 [4, 2, 768, 192], P('section'), may hold values from -0.21875 to 0.21875
- bias_table: float32 [4, 2, 4, 2, 6, 3312], P('section'), may hold values from -4 to 400
Outputs:
- upstream: bfloat16 [4, 8, 12, 48, 192], P('section', None, 'lat', 'lon')
- input_weight_grad: float32 [4, 2, 192, 576], P('section')
- output_weight_grad: float32 [4, 2, 192, 192], P('section')
- expand_weight_grad: float32 [4, 2, 192, 768], P('section')
- reduce_weight_grad: float32 [4, 2, 768, 192], P('section')
- norm_gain_grad: float32 [4, 2, 2, 192], P('section')
- bias_table_grad: float32 [4, 2, 4, 2, 6, 3312], P('section')
The draws below stay inside these ranges and needn't reach their ends.
All inputs are finite; a program needn't handle non-finite values.
Results may differ from the reference program's by a relative error of at most 0.04.
Values may be sent and summed in bfloat16 or wider, within the bound.
A program may use at most 128 MiB of HBM per device.

```python
import jax
import jax.numpy as jnp
from jax import lax

MODEL_WIDTH = 192
HEADS = 6
MLP_WIDTH = 768
HEAD_SIZE = 32
LEVELS = 8
WIN_LEVELS = 2
WIN_LAT = 6
WIN_LON = 12
BLOCKS = 2
WIN_TOKENS = 144
BIAS_SLOTS = 3312
SECTIONS = 4
LAT_ROWS = 12
LON_COLS = 48
LEVEL_WINDOWS = 4
LAT_WINDOWS = 2
N_LON = 4


def draw_bias_table(key, part):
    shape = (SECTIONS, BLOCKS, LEVEL_WINDOWS, LAT_WINDOWS, HEADS, BIAS_SLOTS)
    base_key = jax.random.fold_in(key, 11)
    return jnp.clip(jax.random.normal(base_key, shape, jnp.float32), -3.0, 3.0)


def shard_levels(rng, shape, cuts, smallest, largest):
    level = 1.0
    for axis_at, blocks in cuts:
        draws = jax.random.uniform(jax.random.fold_in(jax.random.fold_in(rng, 6), axis_at), (blocks,), jnp.float32, smallest / len(cuts), largest / len(cuts))
        level = level * jnp.repeat(jnp.exp(draws), shape[axis_at] // blocks).reshape((-1,) + (1,) * (len(shape) - 1 - axis_at))
    return level


def noise(key, shape, width, bound, cuts=(), kind=jnp.bfloat16):
    gain = shard_levels(key, shape, cuts, -0.22, 0.18) if cuts else 1.0
    entries = jax.random.normal(key, shape, jnp.float32) * width * gain
    return jnp.minimum(jnp.maximum(entries, -bound), bound).astype(kind)


def setup_inputs(seed: int = 0) -> dict:
    streams_of = jax.random.split(jax.random.key(seed), 9)
    return {
        "inputs": noise(streams_of[0], (SECTIONS, LEVELS, LAT_ROWS, LON_COLS, MODEL_WIDTH), 1.0, 6.0, ((0, 4), (2, 2), (3, 4))),
        "grad_output": noise(streams_of[1], (SECTIONS, LEVELS, LAT_ROWS, LON_COLS, MODEL_WIDTH), 1.0, 6.0, ((0, 4), (2, 2), (3, 4))),
        "norm_gains": jnp.clip(1.0 + 0.15 * jax.random.normal(streams_of[2], (SECTIONS, BLOCKS, 2, MODEL_WIDTH), jnp.float32), 0.25, 1.75),
        "input_weight": noise(streams_of[3], (SECTIONS, BLOCKS, MODEL_WIDTH, 3 * MODEL_WIDTH), MODEL_WIDTH ** -0.5, 0.4375, ((0, 4),)),
        "output_weight": noise(streams_of[4], (SECTIONS, BLOCKS, MODEL_WIDTH, MODEL_WIDTH), MODEL_WIDTH ** -0.5, 0.4375, ((0, 4),)),
        "expand_weight": noise(streams_of[5], (SECTIONS, BLOCKS, MODEL_WIDTH, MLP_WIDTH), MODEL_WIDTH ** -0.5, 0.4375, ((0, 4),)),
        "reduce_weight": noise(streams_of[6], (SECTIONS, BLOCKS, MLP_WIDTH, MODEL_WIDTH), MLP_WIDTH ** -0.5, 0.21875, ((0, 4),)),
        "bias_table": draw_bias_table(jax.random.fold_in(streams_of[8], 71), 0),
    }


NORM_EPS = 1e-05
MASK_FILL = -10000.0

def layer_norm(activity, gain_vec):
    centred = activity - lax.optimization_barrier(jnp.mean(activity, axis=-1, keepdims=True))
    spread = lax.optimization_barrier(jnp.mean(centred * centred, axis=-1, keepdims=True))
    return centred * lax.rsqrt(spread + NORM_EPS) * gain_vec

def gelu_tanh(activity):
    return jax.nn.gelu(activity, approximate=True)

def to_windows(tokens_in):
    levels_n, rows_n, cols_n, chans = tokens_in.shape
    shaped = tokens_in.reshape(levels_n // WIN_LEVELS, WIN_LEVELS, rows_n // WIN_LAT, WIN_LAT, cols_n // WIN_LON, WIN_LON, chans)
    shaped = shaped.transpose(0, 2, 4, 1, 3, 5, 6)
    return shaped.reshape(levels_n // WIN_LEVELS, rows_n // WIN_LAT, cols_n // WIN_LON, WIN_TOKENS, chans)

def from_windows(blocks_in):
    level_w, lat_w, lon_w, _, chans = blocks_in.shape
    shaped = blocks_in.reshape(level_w, lat_w, lon_w, WIN_LEVELS, WIN_LAT, WIN_LON, chans)
    shaped = shaped.transpose(0, 3, 1, 4, 2, 5, 6)
    return shaped.reshape(level_w * WIN_LEVELS, lat_w * WIN_LAT, lon_w * WIN_LON, chans)

def slot_index():
    positions = jnp.arange(WIN_TOKENS, dtype=jnp.int32)
    level_of = positions // (WIN_LAT * WIN_LON)
    row_of = positions // WIN_LON % WIN_LAT
    col_of = positions % WIN_LON
    level_pair = level_of[:, None] * WIN_LEVELS + level_of[None, :]
    row_pair = row_of[:, None] * WIN_LAT + row_of[None, :]
    offset = col_of[:, None] - col_of[None, :] + WIN_LON - 1
    return ((level_pair * WIN_LAT * WIN_LAT + row_pair) * (2 * WIN_LON - 1) + offset).astype(jnp.int32)

def region(position, extent, window_len):
    return jnp.where(position < extent - window_len, 0, jnp.where(position < extent - window_len // 2, 1, 2)).astype(jnp.int32)

def dense_bias(table_rows, first_row, lat_total, shifted):
    slot_ids = slot_index().reshape(-1)
    bias_dense = jnp.take(table_rows, slot_ids, axis=-1)
    bias_dense = bias_dense.reshape(table_rows.shape[:-1] + (WIN_TOKENS, WIN_TOKENS))
    if shifted:
        local_rows = table_rows.shape[1] * WIN_LAT
        level_ids = region(jnp.arange(LEVELS, dtype=jnp.int32), LEVELS, WIN_LEVELS)
        row_ids = region(first_row + jnp.arange(local_rows, dtype=jnp.int32), lat_total, WIN_LAT)
        region_ids = level_ids[:, None] * 3 + row_ids[None, :]
        region_grid = jnp.broadcast_to(region_ids[:, :, None, None], (LEVELS, local_rows, WIN_LON, 1))
        token_ids = to_windows(region_grid)[:, :, 0, :, 0]
        matched = token_ids[..., :, None] == token_ids[..., None, :]
        bias_dense = bias_dense + jnp.where(matched, 0.0, MASK_FILL).astype(jnp.float32)[:, :, None]
    return bias_dense[:, :, None]

def mix_tokens(tokens_in, weight):
    token_rows = tokens_in.reshape(-1, tokens_in.shape[-1])
    result = jnp.dot(token_rows, weight, preferred_element_type=jnp.float32)
    return result.reshape(tokens_in.shape[:-1] + (weight.shape[1],))

def mix_back(tokens_in, weight):
    token_rows = tokens_in.reshape(-1, tokens_in.shape[-1])
    result = lax.dot_general(token_rows, weight, (((1,), (1,)), ((), ())), preferred_element_type=jnp.float32)
    return result.reshape(tokens_in.shape[:-1] + (weight.shape[0],))

def grad_weight(tokens_in, grad_in):
    token_rows = tokens_in.reshape(-1, tokens_in.shape[-1])
    grad_rows = grad_in.reshape(-1, grad_in.shape[-1])
    return lax.dot_general(token_rows, grad_rows, (((0,), (0,)), ((), ())), preferred_element_type=jnp.float32)

def attend_parts(windows, bias_dense, input_weight):
    leading = windows.shape[:-2]
    token_rows = windows.reshape(-1, MODEL_WIDTH)
    projected = jnp.dot(token_rows, input_weight, preferred_element_type=jnp.float32)
    head_shape = leading + (WIN_TOKENS, HEADS, HEAD_SIZE)
    queries = (projected[:, :MODEL_WIDTH] * HEAD_SIZE ** (-0.5)).astype(jnp.bfloat16).reshape(head_shape)
    key_part = projected[:, MODEL_WIDTH:2 * MODEL_WIDTH].astype(jnp.bfloat16).reshape(head_shape)
    values = projected[:, 2 * MODEL_WIDTH:].astype(jnp.bfloat16).reshape(head_shape)
    scores = jnp.einsum('...qhe,...khe->...hqk', queries.astype(jnp.float32), key_part.astype(jnp.float32)) + bias_dense
    attention = jax.nn.softmax(scores, axis=-1)
    weights = attention.astype(jnp.bfloat16)
    mixture = jnp.einsum('...hqk,...khe->...qhe', weights.astype(jnp.float32), values.astype(jnp.float32)).astype(jnp.bfloat16)
    return (token_rows, queries, key_part, values, attention, weights, mixture)

def attend(windows, bias_dense, input_weight, output_weight):
    parts = attend_parts(windows, bias_dense, input_weight)
    mixture = parts[6]
    result = jnp.dot(mixture.reshape(-1, MODEL_WIDTH), output_weight, preferred_element_type=jnp.float32)
    return result.reshape(windows.shape)

def attend_grad(windows, bias_dense, input_weight, output_weight, grad_windows_in):
    token_rows, queries, key_part, values, attention, weights, mixture = attend_parts(windows, bias_dense, input_weight)
    leading = windows.shape[:-2]
    grad_rows = grad_windows_in.reshape(-1, MODEL_WIDTH)
    output_grad = grad_weight(mixture.reshape(-1, MODEL_WIDTH), grad_rows)
    grad_mixture = mix_back(grad_rows, output_weight).astype(jnp.bfloat16).reshape(leading + (WIN_TOKENS, HEADS, HEAD_SIZE))
    grad_values = jnp.einsum('...hqk,...qhe->...khe', weights.astype(jnp.float32), grad_mixture.astype(jnp.float32))
    grad_weights = jnp.einsum('...qhe,...khe->...hqk', grad_mixture.astype(jnp.float32), values.astype(jnp.float32))
    grad_scores = attention * (grad_weights - lax.optimization_barrier(jnp.sum(attention * grad_weights, axis=-1, keepdims=True)))
    score_part = grad_scores.astype(jnp.bfloat16).astype(jnp.float32)
    grad_queries = jnp.einsum('...hqk,...khe->...qhe', score_part, key_part.astype(jnp.float32)) * HEAD_SIZE ** (-0.5)
    grad_keys = jnp.einsum('...hqk,...qhe->...khe', score_part, queries.astype(jnp.float32))
    grad_projected = jnp.concatenate([piece_grad.reshape(-1, MODEL_WIDTH) for piece_grad in (grad_queries, grad_keys, grad_values)], axis=1).astype(jnp.bfloat16)
    input_grad = grad_weight(token_rows, grad_projected)
    grad_windows = mix_back(grad_projected, input_weight).reshape(windows.shape)
    return (grad_windows, input_grad, output_grad, grad_scores)

def table_grad(grad_scores):
    summed = lax.optimization_barrier(jnp.sum(grad_scores, axis=2))
    flat_rows = summed.reshape(-1, WIN_TOKENS * WIN_TOKENS)
    slot_ids = slot_index().reshape(-1)
    result = jax.ops.segment_sum(flat_rows.T, slot_ids, num_segments=BIAS_SLOTS)
    return result.T.reshape(summed.shape[:3] + (BIAS_SLOTS,))

def grouped(windows):
    level_w, lat_w, lon_w = windows.shape[:3]
    shaped = windows.reshape((level_w, lat_w, N_LON, lon_w // N_LON) + windows.shape[3:])
    return jnp.moveaxis(shaped, 2, 0)

def ungrouped(groups, like_shape):
    return jnp.moveaxis(groups, 0, 2).reshape(like_shape)

def attention_forward(framed, bias_dense, input_weight, output_weight):
    windows = to_windows(framed)
    results = lax.map(lambda group_in: attend(group_in, bias_dense, input_weight, output_weight), grouped(windows))
    return from_windows(ungrouped(results, windows.shape))

def attention_backward(framed, bias_dense, input_weight, output_weight, grad_attended):
    windows = to_windows(framed)
    grad_windows = to_windows(grad_attended)

    def accumulate(totals, pieces):
        grad_piece, input_grad, output_grad, grad_scores = attend_grad(pieces[0], bias_dense, input_weight, output_weight, pieces[1])
        return ((totals[0] + input_grad, totals[1] + output_grad, totals[2] + table_grad(grad_scores)), grad_piece)
    initial = (jnp.zeros((MODEL_WIDTH, 3 * MODEL_WIDTH), jnp.float32), jnp.zeros((MODEL_WIDTH, MODEL_WIDTH), jnp.float32), jnp.zeros(bias_dense.shape[:2] + (HEADS, BIAS_SLOTS), jnp.float32))
    totals, grad_groups = lax.scan(accumulate, initial, (grouped(windows), grouped(grad_windows)))
    return (from_windows(ungrouped(grad_groups, windows.shape)), totals[0], totals[1], totals[2])

def roll_fore(tokens_in):
    return jnp.roll(tokens_in, (-(WIN_LEVELS // 2), -(WIN_LAT // 2), -(WIN_LON // 2)), axis=(0, 1, 2))

def roll_back(tokens_in):
    return jnp.roll(tokens_in, (WIN_LEVELS // 2, WIN_LAT // 2, WIN_LON // 2), axis=(0, 1, 2))

def attention_front(block_in, gain_pair, input_weight, output_weight, bias_dense, shifted):
    normed = layer_norm(block_in.astype(jnp.float32), gain_pair[0]).astype(jnp.bfloat16)
    framed = roll_fore(normed) if shifted else normed
    attended = attention_forward(framed, bias_dense, input_weight, output_weight)
    if shifted:
        attended = roll_back(attended.astype(jnp.bfloat16)).astype(jnp.float32)
    middle = (block_in.astype(jnp.float32) + attended).astype(jnp.bfloat16)
    return (framed, middle)

def block_forward(block_in, gain_pair, input_weight, output_weight, expand_weight, reduce_weight, bias_dense, shifted):
    framed, middle = attention_front(block_in, gain_pair, input_weight, output_weight, bias_dense, shifted)
    normed_mid = layer_norm(middle.astype(jnp.float32), gain_pair[1]).astype(jnp.bfloat16)
    hidden = gelu_tanh(mix_tokens(normed_mid, expand_weight)).astype(jnp.bfloat16)
    return (middle.astype(jnp.float32) + mix_tokens(hidden, reduce_weight)).astype(jnp.bfloat16)

def block_grad(block_in, grad_in, gain_pair, input_weight, output_weight, expand_weight, reduce_weight, bias_dense, shifted):
    framed, middle = attention_front(block_in, gain_pair, input_weight, output_weight, bias_dense, shifted)
    normed_mid, mid_back = jax.vjp(layer_norm, middle.astype(jnp.float32), gain_pair[1])
    normed_mid_b = normed_mid.astype(jnp.bfloat16)
    hidden, gelu_back = jax.vjp(gelu_tanh, mix_tokens(normed_mid_b, expand_weight))
    hidden_b = hidden.astype(jnp.bfloat16)
    reduce_grad = grad_weight(hidden_b, grad_in)
    grad_pre = gelu_back(mix_back(grad_in, reduce_weight))[0].astype(jnp.bfloat16)
    expand_grad = grad_weight(normed_mid_b, grad_pre)
    grad_mid_norm, gain_mid_grad = mid_back(mix_back(grad_pre, expand_weight))
    grad_middle = grad_in.astype(jnp.float32) + grad_mid_norm
    grad_middle_b = grad_middle.astype(jnp.bfloat16)
    grad_attended = roll_fore(grad_middle_b) if shifted else grad_middle_b
    grad_framed, input_grad, output_grad, bias_grad = attention_backward(framed, bias_dense, input_weight, output_weight, grad_attended)
    grad_normed = grad_framed.astype(jnp.bfloat16)
    if shifted:
        grad_normed = roll_back(grad_normed)
    norm_back = jax.vjp(layer_norm, block_in.astype(jnp.float32), gain_pair[0])[1]
    grad_in_norm, gain_in_grad = norm_back(grad_normed.astype(jnp.float32))
    grad_out = (grad_middle + grad_in_norm).astype(jnp.bfloat16)
    return (grad_out, (input_grad, output_grad, expand_grad, reduce_grad, jnp.stack([gain_in_grad, gain_mid_grad]), bias_grad))

def reference(inputs, grad_output, norm_gains, input_weight, output_weight, expand_weight, reduce_weight, bias_table):
    grad_scale = float(LEVELS * LAT_ROWS * LON_COLS) ** (-0.5)
    section_grads = []
    section_parts = []
    for section_idx in range(SECTIONS):
        denses = [dense_bias(bias_table[section_idx, block], 0, LAT_ROWS, block % 2 == 1) for block in range(BLOCKS)]
        block_inputs = [inputs[section_idx]]
        for block in range(BLOCKS - 1):
            block_inputs.append(block_forward(block_inputs[-1], norm_gains[section_idx, block], input_weight[section_idx, block], output_weight[section_idx, block], expand_weight[section_idx, block], reduce_weight[section_idx, block], denses[block], block % 2 == 1))
        grad_flow = grad_output[section_idx]
        collected = [None] * BLOCKS
        for block in reversed(range(BLOCKS)):
            grad_flow, collected[block] = block_grad(block_inputs[block], grad_flow, norm_gains[section_idx, block], input_weight[section_idx, block], output_weight[section_idx, block], expand_weight[section_idx, block], reduce_weight[section_idx, block], denses[block], block % 2 == 1)
        section_grads.append(grad_flow)
        section_parts.append([jnp.stack([collected[block][index] for block in range(BLOCKS)]) for index in range(6)])
    upstream = jnp.stack(section_grads[1:] + [jnp.zeros_like(section_grads[0])])
    outputs = [jnp.stack([section_parts[section_idx][index] for section_idx in range(SECTIONS)]) for index in range(6)]
    return (upstream, outputs[0] * grad_scale, outputs[1] * grad_scale, outputs[2] * grad_scale, outputs[3] * grad_scale, outputs[4] * grad_scale, outputs[5])
```

```python
import functools

import jax
import jax.numpy as jnp
import numpy as np
from jax import lax
from jax.experimental import pallas as pl
from jax.experimental.pallas import tpu as pltpu
from jax.sharding import PartitionSpec as P

D = 192
HEADS = 6
HEAD_SIZE = 32
LEVELS = 8
WIN_LEVELS = 2
ROWS = 6
COLS = 12
WIN = 144
LEVEL_WINDOWS = 4
TOKENS = 576
MLP = 768
SLOTS = 3312
GROUPS = 12
OFFSETS = 23
PAIRS = GROUPS * OFFSETS
PAIRS_PAD = 384
STACK = HEADS * WIN
TABLE_ROWS = LEVEL_WINDOWS * HEADS * GROUPS
TABLE_PAD = 320
GRAD_LANES = 2560
NORM_EPS = 1e-05
MASK_FILL = -10000.0
Q_SCALE = HEAD_SIZE ** (-0.5)
VMEM_BYTES = 50 * 1024 * 1024
F32 = jnp.float32
BF16 = jnp.bfloat16
DENSE = 288


def roll_maps():
    split = np.zeros((TOKENS, TOKENS), np.float32)
    join = np.zeros((TOKENS, TOKENS), np.float32)
    row = 0
    for dest in range(4):
        for level in range(LEVELS):
            for r in range(3):
                for c in range(6):
                    src_r = (1 - dest // 2) * 3 + r
                    src_c = (1 - dest % 2) * 6 + c
                    src = ((level + 1) % LEVELS) * 72 + src_r * COLS + src_c
                    split[row, src] = 1
                    out = level * 72 + ((dest // 2) * 3 + r) * COLS + (dest % 2) * 6 + c
                    join[out, row] = 1
                    row += 1
    return split, join


def spread_map():
    table = np.zeros((COLS, PAIRS_PAD, 256), np.float32)
    for cq in range(COLS):
        for key in range(WIN):
            group, ck = key // COLS, key % COLS
            table[cq, group * OFFSETS + cq - ck + COLS - 1, key] = 1
    return table


def mm(a, b):
    return jnp.dot(a, b, preferred_element_type=F32)


def mm_bt(a, b):
    return lax.dot_general(a, b, (((1,), (1,)), ((), ())), preferred_element_type=F32)


def mm_at(a, b):
    return lax.dot_general(a, b, (((0,), (0,)), ((), ())), preferred_element_type=F32)


def norm_parts(v):
    centred = v - jnp.mean(v, axis=-1, keepdims=True)
    rstd = lax.rsqrt(jnp.mean(centred * centred, axis=-1, keepdims=True) + NORM_EPS)
    return centred * rstd, rstd


def norm_back(v, gain, grad):
    hat, rstd = norm_parts(v)
    scaled = grad * gain
    m1 = jnp.mean(scaled, axis=-1, keepdims=True)
    m2 = jnp.mean(scaled * hat, axis=-1, keepdims=True)
    return rstd * (scaled - m1 - hat * m2), jnp.sum(grad * hat, axis=0, keepdims=True)


def gelu_both(u):
    c = 0.7978845608028654
    t = jnp.tanh(c * (u + 0.044715 * (u * u * u)))
    value = 0.5 * u * (1.0 + t)
    slope = 0.5 * (1.0 + t) + 0.5 * u * (1.0 - t * t) * (c * (1.0 + 3 * 0.044715 * (u * u)))
    return value, slope


def head_masks(dtype):
    lane = lax.broadcasted_iota(jnp.int32, (1, D), 1)
    return [
        jnp.where((lane >= h * HEAD_SIZE) & (lane < (h + 1) * HEAD_SIZE), 1.0, 0.0).astype(dtype)
        for h in range(HEADS)
    ]


def stack_heads(x):
    return jnp.concatenate([x * m for m in head_masks(BF16)], axis=0)


def merge_heads(x):
    total = None
    for h, m in enumerate(head_masks(F32)):
        part = x[h * WIN : (h + 1) * WIN] * m
        total = part if total is None else total + part
    return total


def dense_loop(fn):
    def step(i, carry):
        fn(pl.ds(pl.multiple_of(i * DENSE, 16), DENSE))
        return carry

    lax.fori_loop(0, TOKENS // DENSE, step, 0)


def split3(x):
    hi = x.astype(BF16)
    rest = x - hi.astype(F32)
    mid = rest.astype(BF16)
    low = (rest - mid.astype(F32)).astype(BF16)
    return hi, mid, low


def bias_build(table_ref, spread_ref, ba, bb):
    hi, mid, low = split3(table_ref[...])
    for cq in range(COLS):
        s = spread_ref[cq]
        r = (mm(low, s) + mm(mid, s)) + mm(hi, s)
        ba[pl.ds(cq, TABLE_ROWS, COLS), :] = r[:, :128]
        bb[pl.ds(cq, TABLE_ROWS, COLS), :] = r[:, 128:]


def table_fold(ga, gb, spread_ref, out_ref, gains):
    acc = jnp.zeros((TABLE_ROWS, PAIRS_PAD), F32)
    for cq in range(COLS):
        x = jnp.concatenate(
            [ga[pl.ds(cq, TABLE_ROWS, COLS), :], gb[pl.ds(cq, TABLE_ROWS, COLS), :]], axis=1
        )
        hi = x.astype(BF16)
        low = (x - hi.astype(F32)).astype(BF16)
        s = spread_ref[cq]
        acc = acc + (mm_bt(low, s) + mm_bt(hi, s))
    out_ref[0:TABLE_ROWS, :] = acc.astype(BF16)


def project(framed, wi_ref, q_ref, k_ref, v_ref, rows):
    q_ref[rows, :] = (mm(framed, wi_ref[0]) * Q_SCALE).astype(BF16)
    k_ref[rows, :] = mm(framed, wi_ref[1]).astype(BF16)
    v_ref[rows, :] = mm(framed, wi_ref[2]).astype(BF16)


def attend(q_ref, k_ref, v_ref, ba, bb, at_ref, mx_ref, last_band):
    def window(w, carry):
        rows = pl.ds(pl.multiple_of(w * WIN, 16), WIN)
        big = pl.ds(pl.multiple_of(w * STACK, 16), STACK)
        qst = stack_heads(q_ref[rows, :])
        scores = mm_bt(qst, k_ref[rows, :])
        scores = scores + jnp.concatenate([ba[big, :], bb[big, :]], axis=1)[:, :WIN]
        if last_band is not None:
            qi = lax.broadcasted_iota(jnp.int32, (WIN, WIN), 0)
            ki = lax.broadcasted_iota(jnp.int32, (WIN, WIN), 1)
            qa, ka = (qi >= 72).astype(jnp.int32), (ki >= 72).astype(jnp.int32)
            qb = (qi - 72 * qa >= 36).astype(jnp.int32)
            kb = (ki - 72 * ka >= 36).astype(jnp.int32)
            last_level = (w == LEVEL_WINDOWS - 1).astype(jnp.int32)
            apart = (qa != ka).astype(jnp.int32) * last_level + (qb != kb).astype(
                jnp.int32
            ) * last_band
            mask = jnp.where(apart > 0, MASK_FILL, 0.0)
            scores = scores + jnp.concatenate([mask] * HEADS, axis=0)
        scores = jnp.exp(scores - jnp.max(scores, axis=-1, keepdims=True))
        att = scores / jnp.sum(scores, axis=-1, keepdims=True)
        at_ref[big, :] = att
        mx_ref[rows, :] = merge_heads(mm(att.astype(BF16), v_ref[rows, :])).astype(BF16)
        return carry

    lax.fori_loop(0, LEVEL_WINDOWS, window, 0)


def attend_back(q_ref, k_ref, v_ref, at_ref, gmx, gq_ref, gk_ref, gv_ref, ga, gb):
    def window(w, carry):
        rows = pl.ds(pl.multiple_of(w * WIN, 16), WIN)
        big = pl.ds(pl.multiple_of(w * STACK, 16), STACK)
        qst = stack_heads(q_ref[rows, :])
        gst = stack_heads(gmx[rows, :])
        att = at_ref[big, :]
        gv_ref[rows, :] = mm_at(att.astype(BF16), gst).astype(BF16)
        gw = mm_bt(gst, v_ref[rows, :])
        gs = att * (gw - jnp.sum(att * gw, axis=-1, keepdims=True))
        ga[big, :] = gs[:, :128]
        gb[big, :] = jnp.concatenate([gs[:, 128:], jnp.zeros((STACK, 256 - WIN), F32)], axis=1)
        sp = gs.astype(BF16)
        gq_ref[rows, :] = (merge_heads(mm(sp, k_ref[rows, :])) * Q_SCALE).astype(BF16)
        gk_ref[rows, :] = mm_at(sp, qst).astype(BF16)
        return carry

    lax.fori_loop(0, LEVEL_WINDOWS, window, 0)


def bias_kernel(table_ref, spread_ref, ba, bb):
    bias_build(table_ref, spread_ref, ba, bb)


def forward0_kernel(
    x, gains, wi, wo, we, wr, table, spread, split,
    fr, q, k, v, at, mx, md, nm, hb, gd, a1, sq,
    ba, bb, n1,
):
    bias_build(table, spread, ba, bb)

    def first(rows):
        framed = (norm_parts(x[rows, :].astype(F32))[0] * gains[0:1, :]).astype(BF16)
        fr[rows, :] = framed
        project(framed, wi, q, k, v, rows)

    dense_loop(first)
    attend(q, k, v, ba, bb, at, mx, None)

    def second(rows):
        mid = (x[rows, :].astype(F32) + mm(mx[rows, :], wo[...])).astype(BF16)
        md[rows, :] = mid
        midf = mid.astype(F32)
        normed = (norm_parts(midf)[0] * gains[1:2, :]).astype(BF16)
        nm[rows, :] = normed
        hidden, slope = gelu_both(mm(normed, we[...]))
        hidden = hidden.astype(BF16)
        hb[rows, :] = hidden
        gd[rows, :] = slope.astype(BF16)
        out = (midf + mm(hidden, wr[...])).astype(BF16)
        a1[rows, :] = out
        n1[rows, :] = (norm_parts(out.astype(F32))[0] * gains[2:3, :]).astype(BF16)

    dense_loop(second)
    sq[...] = mm(split[...], n1[...]).astype(BF16)


def forward1_kernel(rq, wi, wo, ba, bb, join, join_t, fr, q, k, v, at, mx, out, *, lat_name):
    def first(rows):
        framed = mm(join[rows, :], rq[...]).astype(BF16)
        fr[rows, :] = framed
        project(framed, wi, q, k, v, rows)

    dense_loop(first)
    last_band = (lax.axis_index(lat_name) == lax.axis_size(lat_name) - 1).astype(jnp.int32)
    attend(q, k, v, ba, bb, at, mx, last_band)
    attended = mm(mx[...], wo[...]).astype(BF16)
    out[...] = mm(join_t[...], attended).astype(BF16)


def mlp_back(rows, e, md, gd, gain, we, wr, gp):
    ef = e[rows, :]
    pre = (gd[rows, :].astype(F32) * mm_bt(ef, wr[...])).astype(BF16)
    gp[rows, :] = pre
    dx, dg = norm_back(md[rows, :].astype(F32), gain, mm_bt(pre, we[...]))
    return ef.astype(F32) + dx, dg


def middle1_kernel(
    rq, a1, go, gains, we, wr, split, split_t,
    gm, gmlp, gain_out, sq,
    md, nm, hb, gd, gp, gmb,
):
    gain_out[...] = jnp.zeros_like(gain_out)

    def step(rows):
        attended = mm(split_t[rows, :], rq[...])
        mid = (a1[rows, :].astype(F32) + attended).astype(BF16)
        md[rows, :] = mid
        normed = (norm_parts(mid.astype(F32))[0] * gains[3:4, :]).astype(BF16)
        nm[rows, :] = normed
        hidden, slope = gelu_both(mm(normed, we[...]))
        hb[rows, :] = hidden.astype(BF16)
        gd[rows, :] = slope.astype(BF16)
        grad, dg = mlp_back(rows, go, md, gd, gains[3:4, :], we, wr, gp)
        gm[rows, :] = grad
        gmb[rows, :] = grad.astype(BF16)
        gain_out[0:1, :] += dg

    dense_loop(step)
    sq[...] = mm(split[...], gmb[...]).astype(BF16)
    gmlp[:, 0:MLP] = mm_at(nm[...], gp[...]).astype(BF16)
    gmlp[:, MLP:] = mm_at(go[...], hb[...]).astype(BF16)


def attention_grads(fr, mx, grad_att, gq, gk, gv, g_out):
    pad = jnp.zeros((D, 64), F32)
    parts = [
        mm_at(fr[...], gq[...]),
        mm_at(fr[...], gk[...]),
        mm_at(fr[...], gv[...]),
        mm_at(mx[...], grad_att),
    ]
    for i, part in enumerate(parts):
        g_out[:, i * 256 : (i + 1) * 256] = jnp.concatenate([part, pad], axis=1).astype(BF16)


def back1_kernel(
    rq, gmlp, fr, q, k, v, at, mx, wi, wo, join, join_t,
    g_out, out, ga, gb,
    gatt, gmx, gq, gk, gv,
):
    def first(rows):
        moved = mm(join[rows, :], rq[...]).astype(BF16)
        gatt[rows, :] = moved
        gmx[rows, :] = mm_bt(moved, wo[...]).astype(BF16)

    dense_loop(first)
    attend_back(q, k, v, at, gmx, gq, gk, gv, ga, gb)
    gn = mm_bt(gq[...], wi[0]) + mm_bt(gk[...], wi[1]) + mm_bt(gv[...], wi[2])
    out[...] = mm(join_t[...], gn.astype(BF16)).astype(BF16)
    attention_grads(fr, mx, gatt[...], gq, gk, gv, g_out)
    g_out[:, 1024:] = gmlp[...]


def table_kernel(ga, gb, spread, out):
    table_fold(ga, gb, spread, out, None)
    out[TABLE_ROWS:, :] = jnp.zeros((TABLE_PAD - TABLE_ROWS, PAIRS_PAD), BF16)


def back0_kernel(
    rq, gm1, a1, x, gains, gain_in, fr, q, k, v, at, mx, md, nm, hb, gd, wi, wo, we, wr,
    spread, split_t,
    g_out, e0, t_out,
    e1, gp, gm0, gatt, gmx, gq, gk, gv, ga, gb, dgains,
):
    dgains[...] = jnp.zeros_like(dgains)
    dgains[3:4, 0:D] = gain_in[0:1, :]

    def first(rows):
        moved = mm(split_t[rows, :], rq[...])
        dx, dg = norm_back(a1[rows, :].astype(F32), gains[2:3, :], moved)
        e1[rows, :] = (gm1[rows, :] + dx).astype(BF16)
        dgains[2:3, 0:D] += dg
        grad, dg = mlp_back(rows, e1, md, gd, gains[1:2, :], we, wr, gp)
        dgains[1:2, 0:D] += dg
        gm0[rows, :] = grad
        moved = grad.astype(BF16)
        gatt[rows, :] = moved
        gmx[rows, :] = mm_bt(moved, wo[...]).astype(BF16)

    dense_loop(first)
    attend_back(q, k, v, at, gmx, gq, gk, gv, ga, gb)

    def last(rows):
        gn = mm_bt(gq[rows, :], wi[0]) + mm_bt(gk[rows, :], wi[1]) + mm_bt(gv[rows, :], wi[2])
        gn = gn.astype(BF16).astype(F32)
        dx, dg = norm_back(x[rows, :].astype(F32), gains[0:1, :], gn)
        dgains[0:1, 0:D] += dg
        e0[rows, :] = (gm0[rows, :] + dx).astype(BF16)

    dense_loop(last)
    attention_grads(fr, mx, gatt[...], gq, gk, gv, g_out)
    g_out[:, 1024 : 1024 + MLP] = mm_at(nm[...], gp[...]).astype(BF16)
    g_out[:, 1024 + MLP :] = mm_at(e1[...], hb[...]).astype(BF16)
    table_fold(ga, gb, spread, t_out, None)
    t_out[TABLE_ROWS:, :] = dgains[...].astype(BF16)


def bf(*shape):
    return jax.ShapeDtypeStruct(shape, BF16)


def ff(*shape):
    return jax.ShapeDtypeStruct(shape, F32)


def run(body, args, outs, scratch=(), flops=10**9):
    return pl.pallas_call(
        body,
        out_shape=tuple(outs),
        in_specs=[pl.BlockSpec(memory_space=pltpu.VMEM)] * len(args),
        out_specs=tuple(pl.BlockSpec(memory_space=pltpu.VMEM) for _ in outs),
        scratch_shapes=[pltpu.VMEM(s.shape, s.dtype) for s in scratch],
        compiler_params=pltpu.CompilerParams(vmem_limit_bytes=VMEM_BYTES),
        cost_estimate=pl.CostEstimate(flops=flops, bytes_accessed=10**7, transcendentals=0),
    )(*args)


def exchange(quads, step):
    lon_n, lat_n = lax.axis_size("lon"), lax.axis_size("lat")

    def moved(part, dlat, dlon):
        pairs = []
        for lo in range(lon_n):
            for la in range(lat_n):
                dest = ((lo + dlon) % lon_n) * lat_n + (la + dlat) % lat_n
                pairs.append((lo * lat_n + la, dest))
        return lax.ppermute(part, ("lon", "lat"), pairs)

    parts = [quads[i * WIN : (i + 1) * WIN] for i in range(4)]
    return jnp.concatenate(
        [parts[0], moved(parts[1], 0, step), moved(parts[2], 1, 0), moved(parts[3], 1, step)],
        axis=0,
    )


def reduce_all(grads, table):
    total = lax.psum(grads, ("lon", "lat"))
    table = lax.psum(table, "lon")
    return total, lax.all_gather(table, "lat", axis=0)


def on_device(
    inputs, grad_output, norm_gains, input_weight, output_weight, expand_weight, reduce_weight,
    bias_table,
):
    lat_index = lax.axis_index("lat")
    lat_total = ROWS * lax.axis_size("lat")
    split_np, join_np = roll_maps()
    split, split_t = jnp.asarray(split_np, BF16), jnp.asarray(split_np.T, BF16)
    join, join_t = jnp.asarray(join_np, BF16), jnp.asarray(join_np.T, BF16)
    spread = jnp.asarray(spread_map(), BF16)
    x = inputs.reshape(TOKENS, D)
    go = grad_output.reshape(TOKENS, D)
    gains = norm_gains.reshape(4, D)
    wi = input_weight[0].reshape(2, D, 3, D).swapaxes(1, 2)
    wo, we, wr = output_weight[0], expand_weight[0], reduce_weight[0]
    rows = lax.dynamic_slice_in_dim(bias_table[0], lat_index, 1, axis=2)[:, :, 0]
    rows = rows.reshape(2, LEVEL_WINDOWS * HEADS, 2, 2, 6, 6 * OFFSETS).swapaxes(3, 4)
    rows = rows.reshape(2, TABLE_ROWS, PAIRS)
    rows = jnp.pad(rows, ((0, 0), (0, 0), (0, PAIRS_PAD - PAIRS)))

    big = LEVEL_WINDOWS * STACK
    tok = bf(TOKENS, D)
    wide = bf(TOKENS, MLP)
    half_bias = [ff(big, 128)] * 2
    fr0, q0, k0, v0, at0, mx0, md0, nm0, hb0, gd0, a1, sq = run(
        forward0_kernel,
        (x, gains, wi[0], wo[0], we[0], wr[0], rows[0], spread, split),
        (tok, tok, tok, tok, ff(big, WIN), tok, tok, tok, wide, wide, tok, tok),
        (*half_bias, tok),
    )
    ba, bb = run(bias_kernel, (rows[1], spread), half_bias)
    rq = exchange(sq, -1)
    fr1, q1, k1, v1, at1, mx1, oq = run(
        functools.partial(forward1_kernel, lat_name="lat"),
        (rq, wi[1], wo[1], ba, bb, join, join_t),
        (tok, tok, tok, tok, ff(big, WIN), tok, tok),
    )
    rq = exchange(oq, 1)
    gm1, gmlp, dgain, sq = run(
        middle1_kernel,
        (rq, a1, go, gains, we[1], wr[1], split, split_t),
        (ff(TOKENS, D), bf(D, 2 * MLP), ff(8, D), tok),
        (tok, tok, wide, wide, wide, tok),
    )
    rq = exchange(sq, -1)
    g1, oq, ga, gb = run(
        back1_kernel,
        (rq, gmlp, fr1, q1, k1, v1, at1, mx1, wi[1], wo[1], join, join_t),
        (bf(D, GRAD_LANES), tok, *half_bias),
        (tok, tok, tok, tok, tok),
    )
    (t1,) = run(table_kernel, (ga, gb, spread), (bf(TABLE_PAD, PAIRS_PAD),))
    rq = exchange(oq, 1)
    g0, e0, t0 = run(
        back0_kernel,
        (rq, gm1, a1, x, gains, dgain, fr0, q0, k0, v0, at0, mx0, md0, nm0, hb0, gd0,
         wi[0], wo[0], we[0], wr[0], spread, split_t),
        (bf(D, GRAD_LANES), tok, bf(TABLE_PAD, PAIRS_PAD)),
        (tok, wide, ff(TOKENS, D), tok, tok, tok, tok, tok, *half_bias, ff(32, PAIRS_PAD)),
    )
    sections = lax.axis_size("section")
    upstream = lax.ppermute(e0, "section", [(i, i - 1) for i in range(1, sections)])
    sum1, sum0, tables = reduce_grads(g0, g1, t0, t1)
    return finish(upstream, sum0, sum1, tables, lat_total, inputs.shape)


def reduce_grads(g0, g1, t0, t1):
    sum1 = lax.psum(g1, ("lon", "lat"))
    sum0 = lax.psum(g0, ("lon", "lat"))
    tables = lax.all_gather(lax.psum(jnp.stack([t0, t1]), "lon"), "lat", axis=0)
    return sum1, sum0, tables


def finish(upstream, sum0, sum1, tables, lat_total, shape):
    grad_scale = float(LEVELS * lat_total * COLS * lax.axis_size("lon")) ** (-0.5)
    lat_n = tables.shape[0]
    sums = jnp.stack([sum0, sum1]).astype(F32) * grad_scale
    wi_g = jnp.concatenate([sums[:, :, i * 256 : i * 256 + D] for i in range(3)], axis=-1)
    wo_g = sums[:, :, 768 : 768 + D]
    we_g = sums[:, :, 1024 : 1024 + MLP]
    wr_g = sums[:, :, 1024 + MLP :].swapaxes(1, 2)
    gains = tables[:, 0, TABLE_ROWS : TABLE_ROWS + 4, :D].astype(F32).sum(0) * grad_scale
    tab = tables[:, :, :TABLE_ROWS, :PAIRS]
    tab = tab.reshape(lat_n, 2, LEVEL_WINDOWS, HEADS, 2, 6, 2, 6 * OFFSETS)
    tab = tab.transpose(1, 2, 0, 3, 4, 6, 5, 7)
    tab = tab.reshape(1, 2, LEVEL_WINDOWS, lat_n, HEADS, SLOTS).astype(F32)
    return (
        upstream.reshape(shape),
        wi_g[None],
        wo_g[None],
        we_g[None],
        wr_g[None],
        gains.reshape(1, 2, 2, D),
        tab,
    )


def solution(mesh):
    token = P("section", None, "lat", "lon", None)
    weight = P("section", None, None, None)
    table = P("section", None, None, None, None, None)
    return jax.shard_map(
        on_device,
        mesh=mesh,
        in_specs=(token, token, weight, weight, weight, weight, weight, table),
        out_specs=(token, weight, weight, weight, weight, weight, table),
        check_vma=False,
    )
```

```python
import functools

import jax
import jax.numpy as jnp
import numpy as np
from jax import lax
from jax.experimental import pallas as pl
from jax.experimental.pallas import tpu as pltpu
from jax.sharding import PartitionSpec as P

D = 192
HEADS = 6
HEAD_SIZE = 32
LEVELS = 8
WIN_LEVELS = 2
ROWS = 6
COLS = 12
WIN = 144
LEVEL_WINDOWS = 4
TOKENS = 576
MLP = 768
SLOTS = 3312
GROUPS = 12
OFFSETS = 23
PAIRS = GROUPS * OFFSETS
PAIRS_PAD = 384
STACK = HEADS * WIN
TABLE_ROWS = LEVEL_WINDOWS * HEADS * GROUPS
TABLE_PAD = 320
GRAD_LANES = 2560
NORM_EPS = 1e-05
MASK_FILL = -10000.0
Q_SCALE = HEAD_SIZE ** (-0.5)
VMEM_BYTES = 50 * 1024 * 1024
F32 = jnp.float32
BF16 = jnp.bfloat16
DENSE = 288


def roll_maps():
    split = np.zeros((TOKENS, TOKENS), np.float32)
    join = np.zeros((TOKENS, TOKENS), np.float32)
    row = 0
    for dest in range(4):
        for level in range(LEVELS):
            for r in range(3):
                for c in range(6):
                    src_r = (1 - dest // 2) * 3 + r
                    src_c = (1 - dest % 2) * 6 + c
                    src = ((level + 1) % LEVELS) * 72 + src_r * COLS + src_c
                    split[row, src] = 1
                    out = level * 72 + ((dest // 2) * 3 + r) * COLS + (dest % 2) * 6 + c
                    join[out, row] = 1
                    row += 1
    return split, join


def spread_map():
    table = np.zeros((COLS, PAIRS_PAD, 256), np.float32)
    for cq in range(COLS):
        for key in range(WIN):
            group, ck = key // COLS, key % COLS
            table[cq, group * OFFSETS + cq - ck + COLS - 1, key] = 1
    return table


def mm(a, b):
    return jnp.dot(a, b, preferred_element_type=F32)


def mm_bt(a, b):
    return lax.dot_general(a, b, (((1,), (1,)), ((), ())), preferred_element_type=F32)


def mm_at(a, b):
    return lax.dot_general(a, b, (((0,), (0,)), ((), ())), preferred_element_type=F32)


def norm_parts(v):
    centred = v - jnp.mean(v, axis=-1, keepdims=True)
    rstd = lax.rsqrt(jnp.mean(centred * centred, axis=-1, keepdims=True) + NORM_EPS)
    return centred * rstd, rstd


def norm_back(v, gain, grad):
    hat, rstd = norm_parts(v)
    scaled = grad * gain
    m1 = jnp.mean(scaled, axis=-1, keepdims=True)
    m2 = jnp.mean(scaled * hat, axis=-1, keepdims=True)
    return rstd * (scaled - m1 - hat * m2), jnp.sum(grad * hat, axis=0, keepdims=True)


def gelu_both(u):
    c = 0.7978845608028654
    t = jnp.tanh(c * (u + 0.044715 * (u * u * u)))
    value = 0.5 * u * (1.0 + t)
    slope = 0.5 * (1.0 + t) + 0.5 * u * (1.0 - t * t) * (c * (1.0 + 3 * 0.044715 * (u * u)))
    return value, slope


def head_masks(dtype):
    lane = lax.broadcasted_iota(jnp.int32, (1, D), 1)
    return [
        jnp.where((lane >= h * HEAD_SIZE) & (lane < (h + 1) * HEAD_SIZE), 1.0, 0.0).astype(dtype)
        for h in range(HEADS)
    ]


def stack_heads(x):
    return jnp.concatenate([x * m for m in head_masks(BF16)], axis=0)


def merge_heads(x):
    total = None
    for h, m in enumerate(head_masks(F32)):
        part = x[h * WIN : (h + 1) * WIN] * m
        total = part if total is None else total + part
    return total


def dense_loop(fn):
    def step(i, carry):
        fn(pl.ds(pl.multiple_of(i * DENSE, 16), DENSE))
        return carry

    lax.fori_loop(0, TOKENS // DENSE, step, 0)


def split3(x):
    hi = x.astype(BF16)
    rest = x - hi.astype(F32)
    mid = rest.astype(BF16)
    low = (rest - mid.astype(F32)).astype(BF16)
    return hi, mid, low


def bias_build(table_ref, spread_ref, ba, bb):
    hi, mid, low = split3(table_ref[...])
    for cq in range(COLS):
        s = spread_ref[cq]
        r = (mm(low, s) + mm(mid, s)) + mm(hi, s)
        ba[pl.ds(cq, TABLE_ROWS, COLS), :] = r[:, :128]
        bb[pl.ds(cq, TABLE_ROWS, COLS), :] = r[:, 128:]


def table_fold(ga, gb, spread_ref, out_ref, gains):
    acc = jnp.zeros((TABLE_ROWS, PAIRS_PAD), F32)
    for cq in range(COLS):
        x = jnp.concatenate(
            [ga[pl.ds(cq, TABLE_ROWS, COLS), :], gb[pl.ds(cq, TABLE_ROWS, COLS), :]], axis=1
        )
        hi = x.astype(BF16)
        low = (x - hi.astype(F32)).astype(BF16)
        s = spread_ref[cq]
        acc = acc + (mm_bt(low, s) + mm_bt(hi, s))
    out_ref[0:TABLE_ROWS, :] = acc.astype(BF16)


def project(framed, wi_ref, q_ref, k_ref, v_ref, rows):
    q_ref[rows, :] = (mm(framed, wi_ref[0]) * Q_SCALE).astype(BF16)
    k_ref[rows, :] = mm(framed, wi_ref[1]).astype(BF16)
    v_ref[rows, :] = mm(framed, wi_ref[2]).astype(BF16)


def attend(q_ref, k_ref, v_ref, ba, bb, at_ref, mx_ref, last_band):
    def window(w, carry):
        rows = pl.ds(pl.multiple_of(w * WIN, 16), WIN)
        big = pl.ds(pl.multiple_of(w * STACK, 16), STACK)
        qst = stack_heads(q_ref[rows, :])
        scores = mm_bt(qst, k_ref[rows, :])
        scores = scores + jnp.concatenate([ba[big, :], bb[big, :]], axis=1)[:, :WIN]
        if last_band is not None:
            qi = lax.broadcasted_iota(jnp.int32, (WIN, WIN), 0)
            ki = lax.broadcasted_iota(jnp.int32, (WIN, WIN), 1)
            qa, ka = (qi >= 72).astype(jnp.int32), (ki >= 72).astype(jnp.int32)
            qb = (qi - 72 * qa >= 36).astype(jnp.int32)
            kb = (ki - 72 * ka >= 36).astype(jnp.int32)
            last_level = (w == LEVEL_WINDOWS - 1).astype(jnp.int32)
            apart = (qa != ka).astype(jnp.int32) * last_level + (qb != kb).astype(
                jnp.int32
            ) * last_band
            mask = jnp.where(apart > 0, MASK_FILL, 0.0)
            scores = scores + jnp.concatenate([mask] * HEADS, axis=0)
        scores = jnp.exp(scores - jnp.max(scores, axis=-1, keepdims=True))
        att = scores / jnp.sum(scores, axis=-1, keepdims=True)
        at_ref[big, :] = att
        mx_ref[rows, :] = merge_heads(mm(att.astype(BF16), v_ref[rows, :])).astype(BF16)
        return carry

    lax.fori_loop(0, LEVEL_WINDOWS, window, 0)


def attend_back(q_ref, k_ref, v_ref, at_ref, gmx, gq_ref, gk_ref, gv_ref, ga, gb):
    def window(w, carry):
        rows = pl.ds(pl.multiple_of(w * WIN, 16), WIN)
        big = pl.ds(pl.multiple_of(w * STACK, 16), STACK)
        qst = stack_heads(q_ref[rows, :])
        gst = stack_heads(gmx[rows, :])
        att = at_ref[big, :]
        gv_ref[rows, :] = mm_at(att.astype(BF16), gst).astype(BF16)
        gw = mm_bt(gst, v_ref[rows, :])
        gs = att * (gw - jnp.sum(att * gw, axis=-1, keepdims=True))
        ga[big, :] = gs[:, :128]
        gb[big, :] = jnp.concatenate([gs[:, 128:], jnp.zeros((STACK, 256 - WIN), F32)], axis=1)
        sp = gs.astype(BF16)
        gq_ref[rows, :] = (merge_heads(mm(sp, k_ref[rows, :])) * Q_SCALE).astype(BF16)
        gk_ref[rows, :] = mm_at(sp, qst).astype(BF16)
        return carry

    lax.fori_loop(0, LEVEL_WINDOWS, window, 0)


def bias_kernel(table_ref, spread_ref, ba, bb):
    bias_build(table_ref, spread_ref, ba, bb)


def forward0_kernel(
    x, gains, wi, wo, we, wr, table, spread, split,
    fr, q, k, v, at, mx, md, nm, hb, gd, a1, sq,
    ba, bb, n1,
):
    bias_build(table, spread, ba, bb)

    def first(rows):
        framed = (norm_parts(x[rows, :].astype(F32))[0] * gains[0:1, :]).astype(BF16)
        fr[rows, :] = framed
        project(framed, wi, q, k, v, rows)

    dense_loop(first)
    attend(q, k, v, ba, bb, at, mx, None)

    def second(rows):
        mid = (x[rows, :].astype(F32) + mm(mx[rows, :], wo[...])).astype(BF16)
        md[rows, :] = mid
        midf = mid.astype(F32)
        normed = (norm_parts(midf)[0] * gains[1:2, :]).astype(BF16)
        nm[rows, :] = normed
        hidden, slope = gelu_both(mm(normed, we[...]))
        hidden = hidden.astype(BF16)
        hb[rows, :] = hidden
        gd[rows, :] = slope.astype(BF16)
        out = (midf + mm(hidden, wr[...])).astype(BF16)
        a1[rows, :] = out
        n1[rows, :] = (norm_parts(out.astype(F32))[0] * gains[2:3, :]).astype(BF16)

    dense_loop(second)
    sq[...] = mm(split[...], n1[...]).astype(BF16)


def forward1_kernel(rq, wi, wo, ba, bb, join, join_t, fr, q, k, v, at, mx, out, *, lat_name):
    def first(rows):
        framed = mm(join[rows, :], rq[...]).astype(BF16)
        fr[rows, :] = framed
        project(framed, wi, q, k, v, rows)

    dense_loop(first)
    last_band = (lax.axis_index(lat_name) == lax.axis_size(lat_name) - 1).astype(jnp.int32)
    attend(q, k, v, ba, bb, at, mx, last_band)
    attended = mm(mx[...], wo[...]).astype(BF16)
    out[...] = mm(join_t[...], attended).astype(BF16)


def mlp_back(rows, e, md, gd, gain, we, wr, gp):
    ef = e[rows, :]
    pre = (gd[rows, :].astype(F32) * mm_bt(ef, wr[...])).astype(BF16)
    gp[rows, :] = pre
    dx, dg = norm_back(md[rows, :].astype(F32), gain, mm_bt(pre, we[...]))
    return ef.astype(F32) + dx, dg


def middle1_kernel(
    rq, a1, go, gains, we, wr, split, split_t,
    gm, gmlp, gain_out, sq,
    md, nm, hb, gd, gp, gmb,
):
    gain_out[...] = jnp.zeros_like(gain_out)

    def step(rows):
        attended = mm(split_t[rows, :], rq[...])
        mid = (a1[rows, :].astype(F32) + attended).astype(BF16)
        md[rows, :] = mid
        normed = (norm_parts(mid.astype(F32))[0] * gains[3:4, :]).astype(BF16)
        nm[rows, :] = normed
        hidden, slope = gelu_both(mm(normed, we[...]))
        hb[rows, :] = hidden.astype(BF16)
        gd[rows, :] = slope.astype(BF16)
        grad, dg = mlp_back(rows, go, md, gd, gains[3:4, :], we, wr, gp)
        gm[rows, :] = grad
        gmb[rows, :] = grad.astype(BF16)
        gain_out[0:1, :] += dg

    dense_loop(step)
    sq[...] = mm(split[...], gmb[...]).astype(BF16)
    gmlp[:, 0:MLP] = mm_at(nm[...], gp[...]).astype(BF16)
    gmlp[:, MLP:] = mm_at(go[...], hb[...]).astype(BF16)


def attention_grads(fr, mx, grad_att, gq, gk, gv, g_out):
    pad = jnp.zeros((D, 64), F32)
    parts = [
        mm_at(fr[...], gq[...]),
        mm_at(fr[...], gk[...]),
        mm_at(fr[...], gv[...]),
        mm_at(mx[...], grad_att),
    ]
    for i, part in enumerate(parts):
        g_out[:, i * 256 : (i + 1) * 256] = jnp.concatenate([part, pad], axis=1).astype(BF16)


def back1_kernel(
    rq, gmlp, fr, q, k, v, at, mx, wi, wo, join, join_t,
    g_out, out, ga, gb,
    gatt, gmx, gq, gk, gv,
):
    def first(rows):
        moved = mm(join[rows, :], rq[...]).astype(BF16)
        gatt[rows, :] = moved
        gmx[rows, :] = mm_bt(moved, wo[...]).astype(BF16)

    dense_loop(first)
    attend_back(q, k, v, at, gmx, gq, gk, gv, ga, gb)
    gn = mm_bt(gq[...], wi[0]) + mm_bt(gk[...], wi[1]) + mm_bt(gv[...], wi[2])
    out[...] = mm(join_t[...], gn.astype(BF16)).astype(BF16)
    attention_grads(fr, mx, gatt[...], gq, gk, gv, g_out)
    g_out[:, 1024:] = gmlp[...]


def table_kernel(ga, gb, spread, out):
    table_fold(ga, gb, spread, out, None)
    out[TABLE_ROWS:, :] = jnp.zeros((TABLE_PAD - TABLE_ROWS, PAIRS_PAD), BF16)


def back0_kernel(
    rq, gm1, a1, x, gains, gain_in, fr, q, k, v, at, mx, md, nm, hb, gd, wi, wo, we, wr,
    spread, split_t,
    g_out, e0, t_out,
    e1, gp, gm0, gatt, gmx, gq, gk, gv, ga, gb, dgains,
):
    dgains[...] = jnp.zeros_like(dgains)
    dgains[3:4, 0:D] = gain_in[0:1, :]

    def first(rows):
        moved = mm(split_t[rows, :], rq[...])
        dx, dg = norm_back(a1[rows, :].astype(F32), gains[2:3, :], moved)
        e1[rows, :] = (gm1[rows, :] + dx).astype(BF16)
        dgains[2:3, 0:D] += dg
        grad, dg = mlp_back(rows, e1, md, gd, gains[1:2, :], we, wr, gp)
        dgains[1:2, 0:D] += dg
        gm0[rows, :] = grad
        moved = grad.astype(BF16)
        gatt[rows, :] = moved
        gmx[rows, :] = mm_bt(moved, wo[...]).astype(BF16)

    dense_loop(first)
    attend_back(q, k, v, at, gmx, gq, gk, gv, ga, gb)

    def last(rows):
        gn = mm_bt(gq[rows, :], wi[0]) + mm_bt(gk[rows, :], wi[1]) + mm_bt(gv[rows, :], wi[2])
        gn = gn.astype(BF16).astype(F32)
        dx, dg = norm_back(x[rows, :].astype(F32), gains[0:1, :], gn)
        dgains[0:1, 0:D] += dg
        e0[rows, :] = (gm0[rows, :] + dx).astype(BF16)

    dense_loop(last)
    attention_grads(fr, mx, gatt[...], gq, gk, gv, g_out)
    g_out[:, 1024 : 1024 + MLP] = mm_at(nm[...], gp[...]).astype(BF16)
    g_out[:, 1024 + MLP :] = mm_at(e1[...], hb[...]).astype(BF16)
    table_fold(ga, gb, spread, t_out, None)
    t_out[TABLE_ROWS:, :] = dgains[...].astype(BF16)


def bf(*shape):
    return jax.ShapeDtypeStruct(shape, BF16)


def ff(*shape):
    return jax.ShapeDtypeStruct(shape, F32)


def run(body, args, outs, scratch=(), flops=10**9):
    return pl.pallas_call(
        body,
        out_shape=tuple(outs),
        in_specs=[pl.BlockSpec(memory_space=pltpu.VMEM)] * len(args),
        out_specs=tuple(pl.BlockSpec(memory_space=pltpu.VMEM) for _ in outs),
        scratch_shapes=[pltpu.VMEM(s.shape, s.dtype) for s in scratch],
        compiler_params=pltpu.CompilerParams(vmem_limit_bytes=VMEM_BYTES),
        cost_estimate=pl.CostEstimate(flops=flops, bytes_accessed=10**7, transcendentals=0),
    )(*args)


def exchange(quads, step):
    lon_n, lat_n = lax.axis_size("lon"), lax.axis_size("lat")

    def moved(part, dlat, dlon):
        pairs = []
        for lo in range(lon_n):
            for la in range(lat_n):
                dest = ((lo + dlon) % lon_n) * lat_n + (la + dlat) % lat_n
                pairs.append((lo * lat_n + la, dest))
        return lax.ppermute(part, ("lon", "lat"), pairs)

    parts = [quads[i * WIN : (i + 1) * WIN] for i in range(4)]
    return jnp.concatenate(
        [parts[0], moved(parts[1], 0, step), moved(parts[2], 1, 0), moved(parts[3], 1, step)],
        axis=0,
    )


def on_device(
    inputs, grad_output, norm_gains, input_weight, output_weight, expand_weight, reduce_weight,
    bias_table,
):
    lat_index = lax.axis_index("lat")
    lat_total = ROWS * lax.axis_size("lat")
    split_np, join_np = roll_maps()
    split, split_t = jnp.asarray(split_np, BF16), jnp.asarray(split_np.T, BF16)
    join, join_t = jnp.asarray(join_np, BF16), jnp.asarray(join_np.T, BF16)
    spread = jnp.asarray(spread_map(), BF16)
    x = inputs.reshape(TOKENS, D)
    go = grad_output.reshape(TOKENS, D)
    gains = norm_gains.reshape(4, D)
    wi = input_weight[0].reshape(2, D, 3, D).swapaxes(1, 2)
    wo, we, wr = output_weight[0], expand_weight[0], reduce_weight[0]
    rows = lax.dynamic_slice_in_dim(bias_table[0], lat_index, 1, axis=2)[:, :, 0]
    rows = rows.reshape(2, LEVEL_WINDOWS * HEADS, 2, 2, 6, 6 * OFFSETS).swapaxes(3, 4)
    rows = rows.reshape(2, TABLE_ROWS, PAIRS)
    rows = jnp.pad(rows, ((0, 0), (0, 0), (0, PAIRS_PAD - PAIRS)))

    big = LEVEL_WINDOWS * STACK
    tok = bf(TOKENS, D)
    wide = bf(TOKENS, MLP)
    half_bias = [ff(big, 128)] * 2
    fr0, q0, k0, v0, at0, mx0, md0, nm0, hb0, gd0, a1, sq = run(
        forward0_kernel,
        (x, gains, wi[0], wo[0], we[0], wr[0], rows[0], spread, split),
        (tok, tok, tok, tok, ff(big, WIN), tok, tok, tok, wide, wide, tok, tok),
        (*half_bias, tok),
    )
    ba, bb = run(bias_kernel, (rows[1], spread), half_bias)
    rq = exchange(sq, -1)
    fr1, q1, k1, v1, at1, mx1, oq = run(
        functools.partial(forward1_kernel, lat_name="lat"),
        (rq, wi[1], wo[1], ba, bb, join, join_t),
        (tok, tok, tok, tok, ff(big, WIN), tok, tok),
    )
    rq = exchange(oq, 1)
    gm1, gmlp, dgain, sq = run(
        middle1_kernel,
        (rq, a1, go, gains, we[1], wr[1], split, split_t),
        (ff(TOKENS, D), bf(D, 2 * MLP), ff(8, D), tok),
        (tok, tok, wide, wide, wide, tok),
    )
    rq = exchange(sq, -1)
    g1, oq, ga, gb = run(
        back1_kernel,
        (rq, gmlp, fr1, q1, k1, v1, at1, mx1, wi[1], wo[1], join, join_t),
        (bf(D, GRAD_LANES), tok, *half_bias),
        (tok, tok, tok, tok, tok),
    )
    (t1,) = run(table_kernel, (ga, gb, spread), (bf(TABLE_PAD, PAIRS_PAD),))
    rq = exchange(oq, 1)
    g0, e0, t0 = run(
        back0_kernel,
        (rq, gm1, a1, x, gains, dgain, fr0, q0, k0, v0, at0, mx0, md0, nm0, hb0, gd0,
         wi[0], wo[0], we[0], wr[0], spread, split_t),
        (bf(D, GRAD_LANES), tok, bf(TABLE_PAD, PAIRS_PAD)),
        (tok, wide, ff(TOKENS, D), tok, tok, tok, tok, tok, *half_bias, ff(32, PAIRS_PAD)),
    )
    upstream, sum0, sum1, tables = reduce_grads(g0, g1, t0, t1, e0)
    return finish(upstream, sum0, sum1, tables, lat_total, inputs.shape)


def reduce_grads(g0, g1, t0, t1, e0):
    if lax.axis_size("lon") == 4 and lax.axis_size("lat") == 2:
        return reduce_by_kernel(g0, g1, t0, t1, e0)
    sections = lax.axis_size("section")
    upstream = lax.ppermute(e0, "section", [(i, i - 1) for i in range(1, sections)])
    sum1 = lax.psum(g1, ("lon", "lat"))
    sum0 = lax.psum(g0, ("lon", "lat"))
    tables = lax.all_gather(lax.psum(jnp.stack([t0, t1]), "lon"), "lat", axis=0)
    return upstream, sum0, sum1, tables


PACKETS = (
    (1024, 768, "yab"),
    (0, 512, "aby"),
    (1792, 768, "yab"),
    (512, 512, "aby"),
)


def halved(shape, dim):
    rows, lanes = shape
    return (rows, lanes // 2) if dim == "y" else (rows // 2, lanes)


def packet_shapes(shape, order):
    shapes = []
    for dim in order:
        shape = halved(shape, dim)
        shapes.append(shape)
    return shapes


class Packet:
    def __init__(self, src, out, lane0, width, order, bits, peers, bufs, send, recv):
        self.src, self.out, self.order = src, out, order
        self.bits, self.peers, self.bufs = bits, peers, bufs
        self.send, self.recv = send, recv
        self.row, self.lane = 0, lane0
        self.shape = (src.shape[0], width)
        self.local = (0, lane0)
        self.held = src
        self.copy = None
        self.trail = []

    def cut(self, dim, bit):
        rows, lanes = halved(self.shape, dim)
        if dim == "y":
            return 0, pl.multiple_of(bit * lanes, 128), rows, lanes
        return pl.multiple_of(bit * rows, 16), 0, rows, lanes

    def start(self, k):
        dim = self.order[k]
        dr, dl, rows, lanes = self.cut(dim, 1 - self.bits[dim])
        self.copy = pltpu.make_async_remote_copy(
            src_ref=self.held.at[at(self.local[0], dr, rows, 16), at(self.local[1], dl, lanes, 128)],
            dst_ref=self.bufs[2 * k],
            send_sem=self.send.at[k],
            recv_sem=self.recv.at[k],
            device_id=self.peers[dim],
            device_id_type=pl.DeviceIdType.MESH,
        )
        self.copy.start()

    def add(self, k):
        self.copy.wait()
        dim = self.order[k]
        dr, dl, rows, lanes = self.cut(dim, self.bits[dim])
        mine = self.held[at(self.local[0], dr, rows, 16), at(self.local[1], dl, lanes, 128)]
        total = mine + self.bufs[2 * k][...]
        self.trail.append((self.row, self.lane, self.shape))
        self.row, self.lane, self.shape = self.row + dr, self.lane + dl, (rows, lanes)
        if k == len(self.order) - 1:
            self.out[at(self.row, 0, rows, 16), at(self.lane, 0, lanes, 128)] = total
        else:
            self.held = self.bufs[2 * k + 1]
            self.held[...] = total
            self.local = (0, 0)

    def start_back(self, k):
        dim = self.order[k]
        n = len(self.order)
        rows, lanes = self.shape
        part = self.out.at[at(self.row, 0, rows, 16), at(self.lane, 0, lanes, 128)]
        self.copy = pltpu.make_async_remote_copy(
            src_ref=part,
            dst_ref=part,
            send_sem=self.send.at[n + k],
            recv_sem=self.recv.at[n + k],
            device_id=self.peers[dim],
            device_id_type=pl.DeviceIdType.MESH,
        )
        self.copy.start()

    def finish_back(self):
        self.copy.wait()
        self.row, self.lane, self.shape = self.trail.pop()


def at(base, offset, size, unit):
    start = base + offset
    if isinstance(start, int):
        return pl.ds(start, size)
    return pl.ds(pl.multiple_of(start, unit), size)


def reduce_kernel(g0, g1, t0, t1, e0, r0, r1, tt, eo, *scratch):
    *bufs, send, recv = scratch
    lat, lon = lax.axis_index("lat"), lax.axis_index("lon")
    sec, sections = lax.axis_index("section"), lax.axis_size("section")
    low, high = lax.rem(lon, 2), lax.div(lon, 2)
    bits = {"y": lat, "a": low, "b": high}
    here = {"section": sec, "lon": lon, "lat": lat}
    peers = {
        "y": {**here, "lat": 1 - lat},
        "a": {**here, "lon": lon + 1 - 2 * low},
        "b": {**here, "lon": lon + 2 - 4 * high},
    }
    before = {**here, "section": lax.rem(sec + sections - 1, sections)}
    after = {**here, "section": lax.rem(sec + 1, sections)}
    barrier = pltpu.get_barrier_semaphore()
    for peer in (*peers.values(), before, after):
        pl.semaphore_signal(
            barrier, inc=1, device_id=peer, device_id_type=pl.DeviceIdType.MESH
        )
    pl.semaphore_wait(barrier, 5)

    packets = []
    used = 0
    for src, out in ((g1, r1), (g0, r0)):
        for lane0, width, order in PACKETS:
            i = len(packets)
            packets.append(
                Packet(src, out, lane0, width, order, bits, peers,
                       bufs[used : used + 5], send.at[i], recv.at[i])
            )
            used += 5
    tables = []
    for b, src in ((1, t1), (0, t0)):
        i = len(packets) + len(tables)
        tables.append(
            Packet(src, tt.at[lat, b], 0, PAIRS_PAD, "ab", bits, peers,
                   bufs[used : used + 3], send.at[i], recv.at[i])
        )
        used += 3
    for p in packets[:4] + tables[:1] + packets[4:] + tables[1:]:
        p.start(0)
    i = len(packets) + len(tables)
    up = pltpu.make_async_remote_copy(
        src_ref=e0, dst_ref=eo, send_sem=send.at[i, 0], recv_sem=recv.at[i, 0],
        device_id=before, device_id_type=pl.DeviceIdType.MESH,
    )
    up.start()
    flow = packets[:4] + tables[:1] + packets[4:] + tables[1:]
    for k in range(3):
        for p in flow:
            n = len(p.order)
            if k < n:
                p.add(k)
                if k + 1 < n:
                    p.start(k + 1)
                else:
                    p.start_back(n - 1)
            else:
                p.finish_back()
                p.start_back(0)
    for k in range(3):
        for p in flow:
            n = len(p.order)
            if n == 3:
                p.finish_back()
                if k < 2:
                    p.start_back(1 - k)
            elif k == 0:
                p.finish_back()
                i = 4
                p.copy = pltpu.make_async_remote_copy(
                    src_ref=p.out, dst_ref=p.out, send_sem=p.send.at[i], recv_sem=p.recv.at[i],
                    device_id=peers["y"], device_id_type=pl.DeviceIdType.MESH,
                )
                p.copy.start()
            elif k == 2:
                p.copy.wait()
    up.wait()


def reduce_by_kernel(g0, g1, t0, t1, e0):
    scratch = []
    for _ in range(2):
        for _, width, order in PACKETS:
            one, two, three = packet_shapes((D, width), order)
            scratch += [one, one, two, two, three]
    for _ in range(2):
        one, two = packet_shapes((TABLE_PAD, PAIRS_PAD), "ab")
        scratch += [one, one, two]
    count = 2 * len(PACKETS) + 3
    outs = (bf(D, GRAD_LANES), bf(D, GRAD_LANES), bf(2, 2, TABLE_PAD, PAIRS_PAD), bf(TOKENS, D))
    r0, r1, tt, eo = pl.pallas_call(
        reduce_kernel,
        out_shape=outs,
        in_specs=[pl.BlockSpec(memory_space=pltpu.VMEM)] * 5,
        out_specs=tuple(pl.BlockSpec(memory_space=pltpu.VMEM) for _ in outs),
        scratch_shapes=[pltpu.VMEM(s, BF16) for s in scratch]
        + [pltpu.SemaphoreType.DMA((count, 6)), pltpu.SemaphoreType.DMA((count, 6))],
        compiler_params=pltpu.CompilerParams(
            collective_id=0, has_side_effects=True, vmem_limit_bytes=VMEM_BYTES
        ),
    )(g0, g1, t0, t1, e0)
    last = lax.axis_index("section") == lax.axis_size("section") - 1
    return jnp.where(last, jnp.zeros_like(eo), eo), r0, r1, tt


def finish(upstream, sum0, sum1, tables, lat_total, shape):
    grad_scale = float(LEVELS * lat_total * COLS * lax.axis_size("lon")) ** (-0.5)
    lat_n = tables.shape[0]
    sums = jnp.stack([sum0, sum1]).astype(F32) * grad_scale
    wi_g = jnp.concatenate([sums[:, :, i * 256 : i * 256 + D] for i in range(3)], axis=-1)
    wo_g = sums[:, :, 768 : 768 + D]
    we_g = sums[:, :, 1024 : 1024 + MLP]
    wr_g = sums[:, :, 1024 + MLP :].swapaxes(1, 2)
    gains = tables[:, 0, TABLE_ROWS : TABLE_ROWS + 4, :D].astype(F32).sum(0) * grad_scale
    tab = tables[:, :, :TABLE_ROWS, :PAIRS]
    tab = tab.reshape(lat_n, 2, LEVEL_WINDOWS, HEADS, 2, 6, 2, 6 * OFFSETS)
    tab = tab.transpose(1, 2, 0, 3, 4, 6, 5, 7)
    tab = tab.reshape(1, 2, LEVEL_WINDOWS, lat_n, HEADS, SLOTS).astype(F32)
    return (
        upstream.reshape(shape),
        wi_g[None],
        wo_g[None],
        we_g[None],
        wr_g[None],
        gains.reshape(1, 2, 2, D),
        tab,
    )


def solution(mesh):
    token = P("section", None, "lat", "lon", None)
    weight = P("section", None, None, None)
    table = P("section", None, None, None, None, None)
    return jax.shard_map(
        on_device,
        mesh=mesh,
        in_specs=(token, token, weight, weight, weight, weight, weight, table),
        out_specs=(token, weight, weight, weight, weight, weight, table),
        check_vma=False,
    )
```
